32 devices in a mesh: groups: 2 (over y), pair: 4 (over x, core), feat: 4 (over z).
Axes of the slice: x: 2, y: 2, z: 4, core: 2. Of those that a mesh axis runs over, the one named last changes fastest.
Arguments:
- queries: bfloat16 [512, 458752], P(('groups', 'pair'), 'feat'), parts along dimension 0, may hold values from -6 to 6
- store: bfloat16 [1536, 458752], P(('groups', 'pair'), 'feat'), parts along dimension 0, may hold values from -6 to 6
- stored_norms: float32 [1536], P('groups'), parts along dimension 0, may hold values from 0.5 to 5
- norm_index: int32 [1536], P(('groups', 'pair')), parts along dimension 0, may hold values from 0 to 767
- visit_order: int32 [512], P('groups'), parts along dimension 0, may hold values from 0 to 255, each once
Outputs:
- influence: float32 [512, 768], P(('groups', 'feat'), 'pair'), parts along dimension 0
The draws below stay inside these ranges and needn't reach their ends.
There are 2 independent parts, one for each index of `groups`. The reference program is written for one: setup_inputs(seed, part) draws one part's arguments, and reference() takes and returns one part's arrays. A program takes and returns all parts, laid end to end along the dimension named above; each array names one. Nothing has to cross between parts.
Inputs may be any that keep to these rules, and one draw needn't show every extreme that they name: visit_order is a permutation of the query indices.
All inputs are finite; a program needn't handle non-finite values.
Results may differ from the reference program's by a relative error of at most 0.0003.
Values may be sent and summed in bfloat16 or wider, within the bound.
A program may use at most 192 MiB of HBM per device.

```python
import math
import jax
import jax.numpy as jnp
from jax import lax

F = 458752
NQ = 256
PAIRS = 768
NTAB = 768


def set_ends(drawn, stream_key, least, high):
    dims = drawn.shape
    index_at = [jax.random.randint(jax.random.fold_in(stream_key, axis), (), 0, dims[axis]) for axis in range(len(dims))]
    drawn = drawn.at[tuple(index_at)].set(least)
    longest = dims.index(max(dims))
    index_at[longest] = (index_at[longest] + 1) % dims[longest]
    return drawn.at[tuple(index_at)].set(high)


def shard_levels(rng, dims, split, low, high):
    gain = 1.0
    for axis_at, shards_of in split:
        steps = jax.random.uniform(jax.random.fold_in(jax.random.fold_in(rng, 6), axis_at), (shards_of,), jnp.float32, low / len(split), high / len(split))
        gain = gain * jnp.repeat(jnp.exp(steps), dims[axis_at] // shards_of).reshape((-1,) + (1,) * (len(dims) - 1 - axis_at))
    return gain


def scatter_about(key, dims, width, reach, shards=(), dtype=jnp.bfloat16):
    drawn = jax.random.normal(key, dims, jnp.float32) * width
    if len(shards) > 0:
        drawn = shard_levels(key, dims, shards, -0.22, 0.18) * drawn
    return jnp.clip(drawn, min=-reach, max=reach).astype(dtype)


def setup_inputs(seed: int = 0, part: int = 0) -> dict:
    key_list = jax.random.split(jax.random.key(seed), 6)
    part_splits = jax.random.split(jax.random.fold_in(key_list[5], part), 6)
    queries = scatter_about(part_splits[0], (NQ, F), 1.0, 6.0, ((0, 4), (1, 4)))
    store = scatter_about(part_splits[1], (PAIRS, F), 1.0, 6.0, ((0, 4), (1, 4)))
    stored_norms = jnp.clip(jnp.exp(jax.random.uniform(part_splits[2], (NTAB,), jnp.float32, math.log(0.5), math.log(5.0))), 0.5, 5.0)
    norm_index = set_ends(jax.random.randint(part_splits[3], (PAIRS,), 0, NTAB), jax.random.fold_in(part_splits[3], 1), 0, NTAB - 1).astype(jnp.int32)
    visit_order = jax.random.permutation(part_splits[4], NQ).astype(jnp.int32)
    return {"queries": queries, "store": store, "stored_norms": stored_norms, "norm_index": norm_index, "visit_order": visit_order}


def reference(queries, store, stored_norms, norm_index, visit_order):
    raw = lax.dot_general(queries, store, (((1,), (1,)), ((), ())), preferred_element_type=jnp.float32)
    widened = queries.astype(jnp.float32)
    square = lax.optimization_barrier(jnp.sum(widened * widened, axis=1))
    qnorm = jnp.sqrt(square + 1e-06)
    ordered = jnp.take(raw, visit_order, axis=0)
    scale = jnp.take(qnorm, visit_order)[:, None] * jnp.take(stored_norms, norm_index)[None, :]
    return ordered / scale
```

```python
import functools

import jax
import jax.numpy as jnp
from jax import lax
from jax.experimental import pallas as pl
from jax.experimental.pallas import tpu as pltpu
from jax.sharding import PartitionSpec as P

MESH = pl.DeviceIdType.MESH
LANES = 128
TAIL_ROWS = 16
BUFFERS = 4
AHEAD = 12
EXACT = lax.Precision.HIGHEST


def chunk_width(features):
    tiles = features // LANES
    best = max(t for t in range(1, 17) if tiles % t == 0)
    return best * LANES


def kernel(
    chips, feats, width, segments,
    queries, store, table, index, visit, out,
    sib_land, x_land, xs_land, store_buf, own_buf,
    acc_first, acc_last, sq_first, sq_last, full, order, ordered, red_first, red_last, norm,
    store_sem, own_sem, sib_send, sib_recv, x_send, x_recv, xs_send, xs_recv, z_send, z_recv,
):
    rows, features = queries.shape
    pairs = store.shape[0]
    padded = store_buf.shape[1]
    steps = features // width
    nq = full.shape[0]
    owned = nq // feats
    me = lax.axis_index("pair")
    core = lax.rem(me, 2)
    chip = lax.div(me, 2)
    z = lax.axis_index("feat")
    sibling = me + 1 - 2 * core

    def at(i):
        return pl.ds(pl.multiple_of(i * width, width), width)

    def chip_by(j):
        return lax.rem(chip + j + chips, chips)

    barrier = pltpu.get_barrier_semaphore()
    pl.semaphore_signal(barrier, inc=1, device_id={"pair": sibling}, device_id_type=MESH)
    for j in range(1, chips):
        pl.semaphore_signal(
            barrier, inc=1, device_id={"pair": chip_by(j) * 2 + core}, device_id_type=MESH
        )
    for k in range(1, feats):
        pl.semaphore_signal(
            barrier, inc=1, device_id={"feat": lax.rem(z + k, feats)}, device_id_type=MESH
        )
    pl.semaphore_wait(barrier, chips + feats - 1)

    def sib_copy(i):
        return pltpu.make_async_remote_copy(
            queries.at[:, at(i)], sib_land.at[:, at(i)], sib_send.at[i], sib_recv.at[i],
            device_id={"pair": sibling}, device_id_type=MESH,
        )

    def x_copy(s, j, i):
        part = pl.ds(*segments[s])
        return pltpu.make_async_remote_copy(
            queries.at[part, at(i)], x_land.at[j - 1, part, at(i)],
            x_send.at[s, j - 1, i], x_recv.at[s, j - 1, i],
            device_id={"pair": chip_by(j) * 2 + core}, device_id_type=MESH,
        )

    def xs_copy(s, j, i):
        part = pl.ds(*segments[s])
        return pltpu.make_async_remote_copy(
            x_land.at[j - 1, part, at(i)], xs_land.at[j - 1, part, at(i)],
            xs_send.at[s, j - 1, i], xs_recv.at[s, j - 1, i],
            device_id={"pair": sibling}, device_id_type=MESH,
        )

    def store_load(i):
        slot = lax.rem(i, BUFFERS)
        return pltpu.make_async_copy(
            store.at[:, at(i)], store_buf.at[slot, pl.ds(0, pairs)], store_sem.at[slot]
        )

    def own_load(i):
        slot = lax.rem(i, BUFFERS)
        return pltpu.make_async_copy(queries.at[:, at(i)], own_buf.at[slot], own_sem.at[slot])

    def send(s, i):
        for j in range(1, chips):
            x_copy(s, j, i).start()
        if s == 0:
            sib_copy(i).start()

    @pl.loop(0, min(AHEAD, steps))
    def _(i):
        send(0, i)

    for i in range(min(BUFFERS - 1, steps)):
        own_load(i).start()
        store_load(i).start()

    store_buf[:, pairs:, :] = jnp.zeros((BUFFERS, padded - pairs, width), store_buf.dtype)
    entries = table.shape[1]
    chosen = (
        lax.broadcasted_iota(jnp.int32, (entries, pairs), 0) == index[...]
    ).astype(jnp.float32)
    norm[...] = jnp.dot(
        jnp.broadcast_to(table[...], (8, entries)), chosen,
        precision=EXACT, preferred_element_type=jnp.float32,
    )
    order[...] = (
        lax.broadcasted_iota(jnp.int32, (nq, nq), 0) == visit[...]
    ).astype(jnp.float32).T
    for ref in (acc_first, acc_last, sq_first, sq_last, full):
        ref[...] = jnp.zeros_like(ref)

    def run(s, acc, sq):
        part = pl.ds(*segments[s])

        @pl.loop(0, steps + 1)
        def _(i):
            @pl.when(i < steps)
            def _():
                for j in range(1, chips):
                    x_copy(s, j, i).wait_recv()
                    xs_copy(s, j, i).start()

            @pl.when(i + AHEAD < steps)
            def _():
                send(s, i + AHEAD)

            if s + 1 < len(segments):
                @pl.when((i + AHEAD >= steps) & (i < steps) & (i + AHEAD - steps < steps))
                def _():
                    send(s + 1, i + AHEAD - steps)

            @pl.when(i >= 1)
            def _():
                n = i - 1
                slot = lax.rem(n, BUFFERS)

                @pl.when(n + BUFFERS - 1 < steps)
                def _():
                    if s == 0:
                        own_load(n + BUFFERS - 1).start()
                    store_load(n + BUFFERS - 1).start()

                store_load(n).wait()
                if s == 0:
                    own_load(n).wait()
                    sib_copy(n).wait_recv()
                for j in range(1, chips):
                    xs_copy(s, j, n).wait_recv()
                pieces = []
                if s == 0:
                    pieces += [own_buf[slot], sib_land[:, at(n)]]
                for j in range(1, chips):
                    pieces += [x_land[j - 1, part, at(n)], xs_land[j - 1, part, at(n)]]
                piece = jnp.concatenate(pieces, axis=0)
                acc[...] += lax.dot_general(
                    piece, store_buf[slot], (((1,), (1,)), ((), ())),
                    preferred_element_type=jnp.float32,
                )
                total = sq[...]
                for t in range(width // LANES):
                    wide = piece[:, t * LANES : (t + 1) * LANES].astype(jnp.float32)
                    total += wide * wide
                sq[...] = total

    def joined(acc, sq):
        square = jnp.sum(sq[...], axis=1, keepdims=True)
        lane = lax.broadcasted_iota(jnp.int32, acc.shape, 1)
        return jnp.where(lane < pairs, acc[...], square)

    def blocks(s):
        start, count = segments[s]
        found = []
        if s == 0:
            found += [(me, 0, rows), (sibling, 0, rows)]
        for j in range(1, chips):
            source = chip_by(-j) * 2 + core
            found += [(source, start, count), (source + 1 - 2 * core, start, count)]
        return found

    def place(s, value):
        offset = 0
        for block, start, count in blocks(s):
            full[pl.ds(pl.multiple_of(block * rows + start, 16), count)] = value[
                offset : offset + count
            ]
            offset += count

    mine = pl.ds(pl.multiple_of(z * owned, 8), owned)

    def first_copy(k):
        target = lax.rem(z + k, feats)
        return pltpu.make_async_remote_copy(
            ordered.at[pl.ds(pl.multiple_of(target * owned, 8), owned)], red_first.at[k],
            z_send.at[0, k], z_recv.at[0, k],
            device_id={"feat": target}, device_id_type=MESH,
        )

    def last_copy(k):
        return pltpu.make_async_remote_copy(
            red_last.at[0], red_last.at[k], z_send.at[1, k], z_recv.at[1, k],
            device_id={"feat": lax.rem(z + k, feats)}, device_id_type=MESH,
        )

    run(0, acc_first, sq_first)
    for i in range(min(BUFFERS - 1, steps)):
        store_load(i).start()
    place(0, joined(acc_first, sq_first))
    ordered[...] = jnp.dot(
        order[...], full[...], precision=EXACT, preferred_element_type=jnp.float32
    )
    for k in range(1, feats):
        first_copy(k).start()

    run(1, acc_last, sq_last)
    red_last[0] = joined(acc_last, sq_last)
    for k in range(1, feats):
        last_copy(k).start()

    @pl.loop(0, steps)
    def _(i):
        sib_copy(i).wait_send()
        for s in range(len(segments)):
            for j in range(1, chips):
                x_copy(s, j, i).wait_send()
                xs_copy(s, j, i).wait_send()

    total = ordered[mine]
    for k in range(1, feats):
        first_copy(k).wait()
        total += red_first[k]
    full[...] = jnp.zeros_like(full)
    last = red_last[0]
    for k in range(1, feats):
        last_copy(k).wait()
        last += red_last[k]
    place(1, last)
    total += jnp.dot(order[mine], full[...], precision=EXACT, preferred_element_type=jnp.float32)
    query_norm = jnp.sqrt(total[:, pairs : pairs + 1] + 1e-06)
    out[...] = total[:, :pairs] / (query_norm * norm[0:1])


def shards(chips, feats, queries, store, stored_norms, norm_index, visit_order):
    rows, features = queries.shape
    pairs = store.shape[0]
    nq = visit_order.shape[0]
    padded = (pairs // LANES + 1) * LANES
    width = chunk_width(features)
    steps = features // width
    segments = ((0, rows - TAIL_ROWS), (rows - TAIL_ROWS, TAIL_ROWS))
    others = chips - 1
    first = 2 * rows + 2 * others * (rows - TAIL_ROWS)
    last = 2 * others * TAIL_ROWS
    vmem = pl.BlockSpec(memory_space=pltpu.VMEM)
    hbm = pl.BlockSpec(memory_space=pltpu.HBM)
    dma = pltpu.SemaphoreType.DMA
    f32, bf16 = jnp.float32, jnp.bfloat16
    return pl.pallas_call(
        functools.partial(kernel, chips, feats, width, segments),
        out_shape=jax.ShapeDtypeStruct((nq // feats, pairs), f32),
        in_specs=[hbm, hbm, vmem, vmem, vmem],
        out_specs=vmem,
        scratch_shapes=[
            pltpu.VMEM((rows, features), bf16),
            pltpu.VMEM((others, rows, features), bf16),
            pltpu.VMEM((others, rows, features), bf16),
            pltpu.VMEM((BUFFERS, padded, width), bf16),
            pltpu.VMEM((BUFFERS, rows, width), bf16),
            pltpu.VMEM((first, padded), f32),
            pltpu.VMEM((last, padded), f32),
            pltpu.VMEM((first, LANES), f32),
            pltpu.VMEM((last, LANES), f32),
            pltpu.VMEM((nq, padded), f32),
            pltpu.VMEM((nq, nq), f32),
            pltpu.VMEM((nq, padded), f32),
            pltpu.VMEM((feats, nq // feats, padded), f32),
            pltpu.VMEM((feats, last, padded), f32),
            pltpu.VMEM((8, pairs), f32),
            dma((BUFFERS,)),
            dma((BUFFERS,)),
            dma((steps,)),
            dma((steps,)),
            dma((2, others, steps)),
            dma((2, others, steps)),
            dma((2, others, steps)),
            dma((2, others, steps)),
            dma((2, feats)),
            dma((2, feats)),
        ],
        compiler_params=pltpu.CompilerParams(
            collective_id=0, has_side_effects=True, vmem_limit_bytes=60 * 2**20
        ),
    )(
        queries, store, stored_norms.reshape(1, -1), norm_index.reshape(1, -1),
        visit_order.reshape(1, -1),
    )


def solution(mesh):
    return jax.shard_map(
        functools.partial(shards, mesh.shape["pair"] // 2, mesh.shape["feat"]),
        mesh=mesh,
        in_specs=(
            P(("groups", "pair"), "feat"),
            P(("groups", "pair"), "feat"),
            P("groups"),
            P(("groups", "pair")),
            P("groups"),
        ),
        out_specs=P(("groups", "feat"), "pair"),
        check_vma=False,
    )
```

```python
import functools

import jax
import jax.numpy as jnp
from jax import lax
from jax.experimental import pallas as pl
from jax.experimental.pallas import tpu as pltpu
from jax.sharding import PartitionSpec as P

MESH = pl.DeviceIdType.MESH
LANES = 128
TAIL_ROWS = 16
BUFFERS = 4
GROUP = 4
AHEAD = (3, 12)
EXACT = lax.Precision.HIGHEST


def chunk_width(features):
    tiles = features // LANES
    best = max(t for t in range(1, 33) if tiles % t == 0)
    return best * LANES


def kernel(
    chips, feats, width, segments, groups,
    queries, store, table, index, visit, out,
    sib_land, x_land, xs_land, store_buf, own_buf,
    acc_first, acc_last, sq_first, sq_last, full, order, ordered, red_first, red_last, norm,
    store_sem, own_sem, sib_send, sib_recv, x_send, x_recv, xs_send, xs_recv, z_send, z_recv,
):
    rows, features = queries.shape
    pairs = store.shape[0]
    padded = store_buf.shape[1]
    steps = features // width
    nq = full.shape[0]
    owned = nq // feats
    me = lax.axis_index("pair")
    core = lax.rem(me, 2)
    chip = lax.div(me, 2)
    z = lax.axis_index("feat")
    sibling = me + 1 - 2 * core

    def at(i):
        return pl.ds(pl.multiple_of(i * width, width), width)

    def span(s, i):
        wide = width * groups[s]
        return pl.ds(pl.multiple_of(i * wide, width), wide)

    def chip_by(j):
        return lax.rem(chip + j + chips, chips)

    barrier = pltpu.get_barrier_semaphore()
    pl.semaphore_signal(barrier, inc=1, device_id={"pair": sibling}, device_id_type=MESH)
    for j in range(1, chips):
        pl.semaphore_signal(
            barrier, inc=1, device_id={"pair": chip_by(j) * 2 + core}, device_id_type=MESH
        )
    for k in range(1, feats):
        pl.semaphore_signal(
            barrier, inc=1, device_id={"feat": lax.rem(z + k, feats)}, device_id_type=MESH
        )
    pl.semaphore_wait(barrier, chips + feats - 1)

    def sib_copy(i):
        return pltpu.make_async_remote_copy(
            queries.at[:, span(0, i)], sib_land.at[:, span(0, i)], sib_send.at[i], sib_recv.at[i],
            device_id={"pair": sibling}, device_id_type=MESH,
        )

    def x_copy(s, j, i):
        part = pl.ds(*segments[s])
        return pltpu.make_async_remote_copy(
            queries.at[part, span(s, i)], x_land.at[j - 1, part, span(s, i)],
            x_send.at[s, j - 1, i], x_recv.at[s, j - 1, i],
            device_id={"pair": chip_by(j) * 2 + core}, device_id_type=MESH,
        )

    def xs_copy(s, j, i):
        part = pl.ds(*segments[s])
        return pltpu.make_async_remote_copy(
            x_land.at[j - 1, part, span(s, i)], xs_land.at[j - 1, part, span(s, i)],
            xs_send.at[s, j - 1, i], xs_recv.at[s, j - 1, i],
            device_id={"pair": sibling}, device_id_type=MESH,
        )

    def store_load(i):
        slot = lax.rem(i, BUFFERS)
        return pltpu.make_async_copy(
            store.at[:, at(i)], store_buf.at[slot, pl.ds(0, pairs)], store_sem.at[slot]
        )

    def own_load(i):
        slot = lax.rem(i, BUFFERS)
        return pltpu.make_async_copy(queries.at[:, at(i)], own_buf.at[slot], own_sem.at[slot])

    def send(s, i):
        for j in range(1, chips):
            x_copy(s, j, i).start()
        if s == 0:
            sib_copy(i).start()

    ahead = [min(AHEAD[s], steps // groups[s]) for s in range(len(segments))]

    def send_first(s):
        @pl.loop(0, ahead[s])
        def _(i):
            send(s, i)

    send_first(0)

    for i in range(min(BUFFERS - 1, steps)):
        own_load(i).start()
        store_load(i).start()

    store_buf[:, pairs:, :] = jnp.zeros((BUFFERS, padded - pairs, width), store_buf.dtype)
    lines, entries = table.shape
    position = lax.broadcasted_iota(jnp.int32, (entries, pairs), 0)
    norms = jnp.zeros((8, pairs), jnp.float32)
    for line in range(lines):
        norms += jnp.dot(
            jnp.broadcast_to(table[line : line + 1], (8, entries)),
            (position + line * entries == index[...]).astype(jnp.float32),
            precision=EXACT, preferred_element_type=jnp.float32,
        )
    norm[...] = norms
    order[...] = (
        lax.broadcasted_iota(jnp.int32, (nq, nq), 0) == visit[...]
    ).astype(jnp.float32).T
    for ref in (acc_first, acc_last, sq_first, sq_last, full):
        ref[...] = jnp.zeros_like(ref)

    def run(s, acc, sq):
        part = pl.ds(*segments[s])
        group = groups[s]
        copies = steps // group

        @pl.loop(0, steps + 1)
        def _(i):
            @pl.when((i < steps) & (lax.rem(i, group) == 0))
            def _():
                c = lax.div(i, group)
                for j in range(1, chips):
                    x_copy(s, j, c).wait_recv()
                    xs_copy(s, j, c).start()

                @pl.when(c + ahead[s] < copies)
                def _():
                    send(s, c + ahead[s])

                if s + 1 < len(segments):
                    @pl.when(c == copies - ahead[s])
                    def _():
                        send_first(s + 1)

            @pl.when(i >= 1)
            def _():
                n = i - 1
                slot = lax.rem(n, BUFFERS)

                @pl.when(n + BUFFERS - 1 < steps)
                def _():
                    if s == 0:
                        own_load(n + BUFFERS - 1).start()
                    store_load(n + BUFFERS - 1).start()

                store_load(n).wait()
                if s == 0:
                    own_load(n).wait()

                @pl.when(lax.rem(n, group) == 0)
                def _():
                    if s == 0:
                        sib_copy(lax.div(n, group)).wait_recv()
                    for j in range(1, chips):
                        xs_copy(s, j, lax.div(n, group)).wait_recv()

                pieces = []
                if s == 0:
                    pieces += [own_buf[slot], sib_land[:, at(n)]]
                for j in range(1, chips):
                    pieces += [x_land[j - 1, part, at(n)], xs_land[j - 1, part, at(n)]]
                piece = jnp.concatenate(pieces, axis=0)
                acc[...] += lax.dot_general(
                    piece, store_buf[slot], (((1,), (1,)), ((), ())),
                    preferred_element_type=jnp.float32,
                )
                total = sq[...]
                for t in range(width // LANES):
                    wide = piece[:, t * LANES : (t + 1) * LANES].astype(jnp.float32)
                    total += wide * wide
                sq[...] = total

    def joined(acc, sq):
        square = jnp.sum(sq[...], axis=1, keepdims=True)
        lane = lax.broadcasted_iota(jnp.int32, acc.shape, 1)
        return jnp.where(lane < pairs, acc[...], square)

    def blocks(s):
        start, count = segments[s]
        found = []
        if s == 0:
            found += [(me, 0, rows), (sibling, 0, rows)]
        for j in range(1, chips):
            source = chip_by(-j) * 2 + core
            found += [(source, start, count), (source + 1 - 2 * core, start, count)]
        return found

    def place(s, value):
        offset = 0
        for block, start, count in blocks(s):
            full[pl.ds(pl.multiple_of(block * rows + start, 16), count)] = value[
                offset : offset + count
            ]
            offset += count

    mine = pl.ds(pl.multiple_of(z * owned, 8), owned)

    def first_copy(k):
        target = lax.rem(z + k, feats)
        return pltpu.make_async_remote_copy(
            ordered.at[pl.ds(pl.multiple_of(target * owned, 8), owned)], red_first.at[k],
            z_send.at[0, k], z_recv.at[0, k],
            device_id={"feat": target}, device_id_type=MESH,
        )

    def last_copy(k):
        return pltpu.make_async_remote_copy(
            red_last.at[0], red_last.at[k], z_send.at[1, k], z_recv.at[1, k],
            device_id={"feat": lax.rem(z + k, feats)}, device_id_type=MESH,
        )

    def sent(s):
        @pl.loop(0, steps // groups[s])
        def _(i):
            if s == 0:
                sib_copy(i).wait_send()
            for j in range(1, chips):
                x_copy(s, j, i).wait_send()
                xs_copy(s, j, i).wait_send()

    run(0, acc_first, sq_first)
    for i in range(min(BUFFERS - 1, steps)):
        store_load(i).start()
    place(0, joined(acc_first, sq_first))
    ordered[...] = jnp.dot(
        order[...], full[...], precision=EXACT, preferred_element_type=jnp.float32
    )
    for k in range(1, feats):
        first_copy(k).start()

    sent(0)
    run(1, acc_last, sq_last)
    red_last[0] = joined(acc_last, sq_last)
    for k in range(1, feats):
        last_copy(k).start()

    sent(1)
    total = ordered[mine]
    for k in range(1, feats):
        first_copy(k).wait()
        total += red_first[k]
    full[...] = jnp.zeros_like(full)
    last = red_last[0]
    for k in range(1, feats):
        last_copy(k).wait()
        last += red_last[k]
    place(1, last)
    total += jnp.dot(order[mine], full[...], precision=EXACT, preferred_element_type=jnp.float32)
    query_norm = jnp.sqrt(total[:, pairs : pairs + 1] + 1e-06)
    out[...] = total[:, :pairs] / (query_norm * norm[0:1])


def shards(chips, feats, queries, store, stored_norms, norm_index, visit_order):
    rows, features = queries.shape
    pairs = store.shape[0]
    nq = visit_order.shape[0]
    padded = (pairs // LANES + 1) * LANES
    width = chunk_width(features)
    steps = features // width
    segments = ((0, rows - TAIL_ROWS), (rows - TAIL_ROWS, TAIL_ROWS))
    groups = (max(g for g in range(1, GROUP + 1) if steps % g == 0), 1)
    others = chips - 1
    first = 2 * rows + 2 * others * (rows - TAIL_ROWS)
    last = 2 * others * TAIL_ROWS
    entries = stored_norms.shape[0]
    line = LANES if entries % LANES == 0 else entries
    vmem = pl.BlockSpec(memory_space=pltpu.VMEM)
    hbm = pl.BlockSpec(memory_space=pltpu.HBM)
    dma = pltpu.SemaphoreType.DMA
    f32, bf16 = jnp.float32, jnp.bfloat16
    return pl.pallas_call(
        functools.partial(kernel, chips, feats, width, segments, groups),
        out_shape=jax.ShapeDtypeStruct((nq // feats, pairs), f32),
        in_specs=[hbm, hbm, vmem, vmem, vmem],
        out_specs=vmem,
        scratch_shapes=[
            pltpu.VMEM((rows, features), bf16),
            pltpu.VMEM((others, rows, features), bf16),
            pltpu.VMEM((others, rows, features), bf16),
            pltpu.VMEM((BUFFERS, padded, width), bf16),
            pltpu.VMEM((BUFFERS, rows, width), bf16),
            pltpu.VMEM((first, padded), f32),
            pltpu.VMEM((last, padded), f32),
            pltpu.VMEM((first, LANES), f32),
            pltpu.VMEM((last, LANES), f32),
            pltpu.VMEM((nq, padded), f32),
            pltpu.VMEM((nq, nq), f32),
            pltpu.VMEM((nq, padded), f32),
            pltpu.VMEM((feats, nq // feats, padded), f32),
            pltpu.VMEM((feats, last, padded), f32),
            pltpu.VMEM((8, pairs), f32),
            dma((BUFFERS,)),
            dma((BUFFERS,)),
            dma((steps,)),
            dma((steps,)),
            dma((2, others, steps)),
            dma((2, others, steps)),
            dma((2, others, steps)),
            dma((2, others, steps)),
            dma((2, feats)),
            dma((2, feats)),
        ],
        compiler_params=pltpu.CompilerParams(
            collective_id=0, has_side_effects=True, vmem_limit_bytes=60 * 2**20
        ),
    )(
        queries, store, stored_norms.reshape(-1, line), norm_index.reshape(1, -1),
        visit_order.reshape(1, -1),
    )


def solution(mesh):
    return jax.shard_map(
        functools.partial(shards, mesh.shape["pair"] // 2, mesh.shape["feat"]),
        mesh=mesh,
        in_specs=(
            P(("groups", "pair"), "feat"),
            P(("groups", "pair"), "feat"),
            P("groups"),
            P(("groups", "pair")),
            P("groups"),
        ),
        out_specs=P(("groups", "feat"), "pair"),
        check_vma=False,
    )
```
